256 devices in a mesh: modes: 32 (over y, z_hi, x), rows: 8 (over z_lo, core).
Axes of the slice: x: 4, y: 4, z: 8 (z_hi: 2, z_lo: 4; z = z_hi * 4 + z_lo), core: 2. Of those that a mesh axis runs over, the one named last changes fastest.
Arguments:
- fwd_fields: bfloat16 [512, 2, 384, 384], P('modes', None, 'rows'), may hold values from -6 to 6
- bwd_fields: bfloat16 [512, 2, 384, 384], P('modes', None, 'rows'), may hold values from -6 to 6
- wavelength: int32 [512], P('modes'), may hold values from 0 to 2
- kernel_phase: float32 [3, 384, 384], replicated, may hold values from -3.140625 to 3.140625
- mask_phase: float32 [384, 384], P('rows'), may hold values from -3.140625 to 3.140625
Outputs:
- fwd_out: bfloat16 [512, 2, 384, 384], P('modes', None, 'rows')
- new_mask: float32 [2, 384, 384], P(None, 'rows')
- coupling: float32 [2, 512], P(None, 'modes')
The draws below stay inside these ranges and needn't reach their ends.
All inputs are finite; a program needn't handle non-finite values.
Results may differ from the reference program's by a relative error of at most 0.034.
Values may be sent and summed in bfloat16 or wider, within the bound.
No kernel may reach another device: no remote copies, remote signals or barrier semaphores. Data moves between devices by JAX's collectives and lax.ppermute only.
A program may use at most 64 MiB of HBM per device.

```python
import math
import jax
import jax.numpy as jnp
from jax import lax

N = 384
WAVES = 3
FIELDS = 512


def plant(values, rng, least, top_value):
    shape = values.shape
    spot = [jax.random.randint(jax.random.fold_in(rng, axis), (), 0, shape[axis]) for axis in range(len(shape))]
    values = values.at[tuple(spot)].set(least)
    longest = shape.index(max(shape))
    spot[longest] = (spot[longest] + 1) % shape[longest]
    return values.at[tuple(spot)].set(top_value)


def steps_of(rng, dims, cuts, smallest, top_value):
    loudness, own = 1.0, jax.random.fold_in(rng, 6)
    for dim, shards_of in cuts:
        draws = jnp.exp(jax.random.uniform(jax.random.fold_in(own, dim), (shards_of,), jnp.float32, smallest / len(cuts), top_value / len(cuts)))
        loudness = loudness * jnp.repeat(draws, dims[dim] // shards_of).reshape([-1 if axis == dim else 1 for axis in range(len(dims))])
    return loudness


def centred(key, extent, spread, bound, pieces=(), kind=jnp.bfloat16):
    loudness = steps_of(key, extent, pieces, -0.22, 0.18) if pieces else 1.0
    entries = jax.random.normal(key, extent, jnp.float32) * spread * loudness
    return jnp.minimum(jnp.maximum(entries, -bound), bound).astype(kind)


def setup_inputs(seed: int = 0) -> dict:
    keys = jax.random.split(jax.random.key(seed), 6)
    fwd_fields = centred(keys[0], (FIELDS, 2, N, N), 1.0, 6.0, ((0, 32), (2, 8)))
    bwd_fields = centred(keys[1], (FIELDS, 2, N, N), 1.0, 6.0, ((0, 32), (2, 8)))
    wavelength = plant(jax.random.randint(keys[2], (FIELDS,), 0, WAVES), jax.random.fold_in(keys[2], 1), 0, WAVES - 1).astype(jnp.int32)
    kernel_phase = jnp.clip(jax.random.uniform(keys[3], (WAVES, N, N), jnp.float32, -3.140625, 3.140625), -3.140625, 3.140625)
    mask_phase = jnp.clip(jax.random.uniform(keys[4], (N, N), jnp.float32, -3.140625, 3.140625), -3.140625, 3.140625)
    return dict(fwd_fields=fwd_fields, bwd_fields=bwd_fields, wavelength=wavelength, kernel_phase=kernel_phase, mask_phase=mask_phase)


def tables(size):
    index = jnp.arange(size, dtype=jnp.int32)
    field_product = index[:, None] * index[None, :] % size
    angles = field_product.astype(jnp.float32) * (2.0 * math.pi / size)
    scale = 1.0 / math.sqrt(size)
    cosine = jnp.cos(angles) * scale
    sine = jnp.sin(angles) * scale
    forward_propagate = jnp.concatenate([jnp.concatenate([cosine, -sine], 1), jnp.concatenate([sine, cosine], 1)], 0).astype(jnp.bfloat16)
    inverse = jnp.concatenate([jnp.concatenate([cosine, sine], 1), jnp.concatenate([-sine, cosine], 1)], 0).astype(jnp.bfloat16)
    return (forward_propagate, inverse)

def hop(field, phase, sign, forward_propagate, inverse):
    size = field.shape[-1]
    joined = jnp.concatenate([field[0], field[1]], axis=1)
    cols = jnp.dot(joined, forward_propagate, preferred_element_type=jnp.float32).astype(jnp.bfloat16)
    stacked_fields = jnp.concatenate([cols[:, :size], cols[:, size:]], axis=0)
    spectrum = jnp.dot(forward_propagate.T, stacked_fields, preferred_element_type=jnp.float32).astype(jnp.bfloat16)
    real_part = spectrum[:size].astype(jnp.float32)
    imag_part = spectrum[size:].astype(jnp.float32)
    cosine = jnp.cos(phase)
    sine = sign * jnp.sin(phase)
    turned = jnp.concatenate([cosine * real_part - sine * imag_part, sine * real_part + cosine * imag_part], 0).astype(jnp.bfloat16)
    back = jnp.dot(inverse.T, turned, preferred_element_type=jnp.float32).astype(jnp.bfloat16)
    joined = jnp.concatenate([back[:size], back[size:]], axis=1)
    space = jnp.dot(joined, inverse, preferred_element_type=jnp.float32)
    return jnp.stack([space[:, :size], space[:, size:]])

def reference(fwd_fields, bwd_fields, wavelength, kernel_phase, mask_phase):
    forward_propagate, inverse = tables(N)

    def both(items):
        fwd_one, bwd_one, wave = items
        phase = lax.dynamic_index_in_dim(kernel_phase, wave, 0, keepdims=False)
        return (hop(fwd_one, phase, 1.0, forward_propagate, inverse), hop(bwd_one, phase, -1.0, forward_propagate, inverse))
    fwd_space, bwd_space = lax.map(both, (fwd_fields, bwd_fields, wavelength))
    fwd_re, fwd_im = (fwd_space[:, 0], fwd_space[:, 1])
    bwd_re, bwd_im = (bwd_space[:, 0], bwd_space[:, 1])
    prod_re = fwd_re * bwd_re + fwd_im * bwd_im
    prod_im = fwd_im * bwd_re - fwd_re * bwd_im
    cosine = jnp.cos(mask_phase)[None]
    sine = jnp.sin(mask_phase)[None]
    coup_re = lax.optimization_barrier(jnp.sum(prod_re * cosine - prod_im * sine, axis=(1, 2))) / N
    coup_im = lax.optimization_barrier(jnp.sum(prod_re * sine + prod_im * cosine, axis=(1, 2))) / N
    scale = 1.0 / math.sqrt(FIELDS)
    high = lax.Precision.HIGHEST
    over_re = (jnp.einsum('fyn,f->yn', prod_re, coup_re, precision=high) + jnp.einsum('fyn,f->yn', prod_im, coup_im, precision=high)) * scale
    over_im = (jnp.einsum('fyn,f->yn', prod_im, coup_re, precision=high) - jnp.einsum('fyn,f->yn', prod_re, coup_im, precision=high)) * scale
    denom = jnp.maximum(jnp.sqrt(over_re * over_re + over_im * over_im), 1.0)
    unit_re = over_re / denom
    unit_im = over_im / denom
    output_real = fwd_re * unit_re[None] - fwd_im * unit_im[None]
    out_im = fwd_re * unit_im[None] + fwd_im * unit_re[None]
    fwd_out = jnp.stack([output_real, out_im], axis=1).astype(jnp.bfloat16)
    new_mask = jnp.stack([unit_re, unit_im])
    coupling = jnp.stack([coup_re, coup_im])
    return (fwd_out, new_mask, coupling)
```

```python
import functools
import math

import jax
import jax.numpy as jnp
from jax import lax
from jax.experimental import pallas as pl
from jax.experimental.pallas import tpu as pltpu
from jax.sharding import PartitionSpec as P

N = 384
ROWS = 8
PIECE = N // ROWS
MINE = 2
HALF = PIECE // 2
FIELDS = 512
X_STEPS = (1, 2, 3)
YZ_STEPS = (4, 8, 12, 16, 20, 24, 28)
VMEM = pl.BlockSpec(memory_space=pltpu.VMEM)
SMEM = pl.BlockSpec(memory_space=pltpu.SMEM)
LIMIT = 50 * 1024 * 1024


def sincos(angle):
    y = angle * 0.5
    z = y * y
    s = -1.0 / 39916800.0
    for c in (1.0 / 362880.0, -1.0 / 5040.0, 1.0 / 120.0, -1.0 / 6.0, 1.0):
        s = s * z + c
    s = s * y
    c = 1.0 / 479001600.0
    for d in (-1.0 / 3628800.0, 1.0 / 40320.0, -1.0 / 720.0, 1.0 / 24.0, -0.5, 1.0):
        c = c * z + d
    return 1.0 - 2.0 * s * s, 2.0 * s * c


def tables_kernel(at_ref, wave_ref, phase_ref, fore_ref, back_ref, trig_ref):
    for r in range(0, N, 128):
        j = lax.broadcasted_iota(jnp.int32, (128, N), 0) + r
        k = lax.broadcasted_iota(jnp.int32, (128, N), 1)
        jk = (j * k).astype(jnp.float32)
        turn = jnp.floor(jk * (1.0 / N) + 0.5)
        cosine, sine = sincos((jk - turn * N) * (2.0 * math.pi / N))
        scale = 1.0 / math.sqrt(N)
        cosine = (cosine * scale).astype(jnp.bfloat16)
        sine = (sine * scale).astype(jnp.bfloat16)
        a, b = pl.ds(r, 128), pl.ds(N + r, 128)
        fore_ref[a, :N] = cosine
        fore_ref[a, N:] = -sine
        fore_ref[b, :N] = sine
        fore_ref[b, N:] = cosine
        back_ref[a, :N] = cosine
        back_ref[a, N:] = sine
        back_ref[b, :N] = -sine
        back_ref[b, N:] = cosine
    for f in range(MINE):
        wave = wave_ref[at_ref[0] * MINE + f]
        for r in range(0, N, 128):
            cosine, sine = sincos(phase_ref[wave, pl.ds(r, 128), :])
            trig_ref[f, 0, pl.ds(r, 128), :] = cosine
            trig_ref[f, 1, pl.ds(r, 128), :] = sine


def dot(a, b):
    return jnp.dot(a, b, preferred_element_type=jnp.float32)


def hop(sign, at_ref, blocks, fore_ref, back_ref, trig_ref, one, two):
    for k in range(ROWS):
        top = pl.multiple_of((at_ref[0] ^ k) * PIECE, 16)
        for f in range(MINE):
            for c in range(2):
                one[pl.ds(f * N + top, PIECE), c * N : (c + 1) * N] = blocks[k][2 * f + c]
    for f in range(MINE):
        a = dot(one[f * N : (f + 1) * N, :], fore_ref[...]).astype(jnp.bfloat16)
        two[:N, f * N : (f + 1) * N] = a[:, :N]
        two[N:, f * N : (f + 1) * N] = a[:, N:]
    for c in range(2):
        one[c * N : (c + 1) * N, :] = dot(back_ref[c * N : (c + 1) * N, :], two[...]).astype(
            jnp.bfloat16
        )
    for f in range(MINE):
        lanes = slice(f * N, (f + 1) * N)
        re = one[:N, lanes].astype(jnp.float32)
        im = one[N:, lanes].astype(jnp.float32)
        cosine, sine = trig_ref[f, 0], sign * trig_ref[f, 1]
        two[:N, lanes] = (cosine * re - sine * im).astype(jnp.bfloat16)
        two[N:, lanes] = (sine * re + cosine * im).astype(jnp.bfloat16)
    for c in range(2):
        d = dot(fore_ref[c * N : (c + 1) * N, :], two[...]).astype(jnp.bfloat16)
        for f in range(MINE):
            one[f * N : (f + 1) * N, c * N : (c + 1) * N] = d[:, f * N : (f + 1) * N]
    return [dot(one[f * N : (f + 1) * N, :], back_ref[...]) for f in range(MINE)]


def forward_kernel(*refs):
    at_ref, blocks = refs[0], refs[1 : 1 + ROWS]
    fore_ref, back_ref, trig_ref, space_ref, out_ref, mask_ref, one, two = refs[1 + ROWS :]
    for k in range(ROWS):
        piece = at_ref[0] ^ k
        cosine, sine = sincos(blocks[k][2 * MINE].astype(jnp.float32))
        mask_ref[0, piece] = cosine
        mask_ref[1, piece] = sine
    space = hop(1.0, at_ref, blocks, fore_ref, back_ref, trig_ref, one, two)
    for f in range(MINE):
        space_ref[f] = space[f]
        low = space[f].astype(jnp.bfloat16)
        for c in range(2):
            out_ref[:, 2 * f + c] = low[:, c * N : (c + 1) * N].reshape(ROWS, PIECE, N)


def total(x):
    return jnp.sum(jnp.sum(x, axis=0, keepdims=True), axis=1, keepdims=True)


def backward_kernel(*refs):
    at_ref, blocks = refs[0], refs[1 : 1 + ROWS]
    fore_ref, back_ref, trig_ref, space_ref, mask_ref, over_ref, coup_ref, one, two = refs[
        1 + ROWS :
    ]
    space = hop(-1.0, at_ref, blocks, fore_ref, back_ref, trig_ref, one, two)
    cosine = mask_ref[0].reshape(N, N)
    sine = mask_ref[1].reshape(N, N)
    over_re, over_im = 0.0, 0.0
    coup_ref[...] = jnp.zeros_like(coup_ref)
    for f in range(MINE):
        b_re, b_im = space[f][:, :N], space[f][:, N:]
        f_re, f_im = space_ref[f, :, :N], space_ref[f, :, N:]
        g_re = f_re * b_re + f_im * b_im
        g_im = f_im * b_re - f_re * b_im
        c_re = total(g_re * cosine - g_im * sine) * (1.0 / N)
        c_im = total(g_re * sine + g_im * cosine) * (1.0 / N)
        over_re = over_re + (g_re * c_re + g_im * c_im)
        over_im = over_im + (g_im * c_re - g_re * c_im)
        for c, value in ((0, c_re), (1, c_im)):
            row = 2 * f + c
            coup_ref[row : row + 1, :] = jnp.broadcast_to(value, (1, 128))
    scale = 1.0 / math.sqrt(FIELDS)
    for c, over in ((0, over_re), (1, over_im)):
        parts = (over * scale).reshape(ROWS, 2, HALF, N)
        for h in range(2):
            over_ref[2 * c + h] = parts[:, h]


def final_kernel(*refs):
    at_ref, parts, blocks = refs[0], refs[1:5], refs[5 : 5 + ROWS]
    out_ref, mask_ref, over = refs[5 + ROWS :]
    for k in range(4):
        over[at_ref[1] ^ k] = parts[k][...]
    re = jnp.concatenate([over[0], over[1]], axis=0)
    im = jnp.concatenate([over[2], over[3]], axis=0)
    denom = jnp.maximum(jnp.sqrt(re * re + im * im), 1.0)
    re, im = re / denom, im / denom
    mask_ref[0] = re
    mask_ref[1] = im
    for k in range(ROWS):
        first = (at_ref[0] ^ k) * MINE
        for f in range(MINE):
            f_re = blocks[k][2 * f].astype(jnp.float32)
            f_im = blocks[k][2 * f + 1].astype(jnp.float32)
            out_ref[first + f, 0] = (f_re * re - f_im * im).astype(jnp.bfloat16)
            out_ref[first + f, 1] = (f_re * im + f_im * re).astype(jnp.bfloat16)


def call(kernel, args, outs, scratch=(), flops=0):
    size = sum(a.size * a.dtype.itemsize for a in args) + sum(
        math.prod(s) * jnp.dtype(t).itemsize for s, t in outs
    )
    return pl.pallas_call(
        kernel,
        out_shape=[jax.ShapeDtypeStruct(s, t) for s, t in outs],
        in_specs=[SMEM if a.dtype == jnp.int32 else VMEM for a in args],
        out_specs=[VMEM] * len(outs),
        scratch_shapes=[pltpu.VMEM(s, t) for s, t in scratch],
        compiler_params=pltpu.CompilerParams(vmem_limit_bytes=LIMIT),
        cost_estimate=pl.CostEstimate(flops=flops, bytes_accessed=size, transcendentals=0),
    )(*args)


def tree(values):
    values = [v.astype(jnp.float32) for v in values]
    while len(values) > 1:
        values = [a + b for a, b in zip(values[::2], values[1::2])]
    return values[0]


def over_rows(block, k):
    return lax.ppermute(block, "rows", [(s, s ^ k) for s in range(ROWS)])


def over_modes(block, k):
    return lax.ppermute(block, "modes", [(s, s ^ k) for s in range(lax.axis_size("modes"))])


def shards(fwd_fields, bwd_fields, wavelength, kernel_phase, mask_phase):
    bf16, f32 = jnp.bfloat16, jnp.float32
    row, mode = lax.axis_index("rows"), lax.axis_index("modes")
    part = mode & 3
    at = jnp.stack([row, part]).astype(jnp.int32)
    low_mask = mask_phase.astype(bf16)[None]

    def fields_for(fields, k):
        block = lax.dynamic_slice_in_dim(fields, (row ^ k) * MINE, MINE, 0)
        return block.reshape(2 * MINE, PIECE, N)

    def exchange(make):
        return [make(0)] + [over_rows(make(k), k) for k in range(1, ROWS)]

    fwd_blocks = exchange(lambda k: jnp.concatenate([fields_for(fwd_fields, k), low_mask], 0))
    bwd_blocks = exchange(lambda k: fields_for(bwd_fields, k))

    fore, back, trig = call(
        tables_kernel,
        [at, wavelength, kernel_phase],
        [((2 * N, 2 * N), bf16), ((2 * N, 2 * N), bf16), ((MINE, 2, N, N), f32)],
    )
    scratch = [((2 * N, 2 * N), bf16), ((2 * N, 2 * N), bf16)]
    work = 4 * 2 * (2 * N) ** 3
    space, outs, mask = call(
        forward_kernel,
        [at, *fwd_blocks, fore, back, trig],
        [((MINE, N, 2 * N), f32), ((ROWS, 2 * MINE, PIECE, N), bf16), ((2, ROWS, PIECE, N), f32)],
        scratch,
        work,
    )
    out_blocks = exchange(lambda k: lax.dynamic_index_in_dim(outs, row ^ k, 0, keepdims=False))
    over, coup = call(
        backward_kernel,
        [at, *bwd_blocks, fore, back, trig, space, mask],
        [((4, ROWS, HALF, N), f32), ((8, 128), f32)],
        scratch,
        work,
    )

    def part_for(k):
        return lax.dynamic_index_in_dim(over, part ^ k, 0, keepdims=False).astype(bf16)

    over = tree([part_for(0)] + [over_modes(part_for(k), k) for k in X_STEPS]).astype(bf16)
    pieces = exchange(lambda k: lax.dynamic_index_in_dim(over, row ^ k, 0, keepdims=False))
    coups = exchange(lambda k: coup)
    over = tree(pieces).astype(bf16)
    over = tree([over] + [over_modes(over, k) for k in YZ_STEPS])
    parts = [over] + [over_modes(over, k) for k in X_STEPS]

    fwd_out, new_mask = call(
        final_kernel,
        [at, *parts, *out_blocks],
        [((ROWS * MINE, 2, PIECE, N), bf16), ((2, PIECE, N), f32)],
        [((4, HALF, N), f32)],
    )
    coups = jnp.stack(coups)[:, : 2 * MINE, 0]
    coups = jnp.stack([lax.dynamic_index_in_dim(coups, row ^ k, 0, False) for k in range(ROWS)])
    coupling = coups.reshape(ROWS, MINE, 2).transpose(2, 0, 1).reshape(2, ROWS * MINE)
    return fwd_out, new_mask, coupling


def solution(mesh):
    in_specs = (
        P("modes", None, "rows", None),
        P("modes", None, "rows", None),
        P("modes"),
        P(),
        P("rows", None),
    )
    out_specs = (P("modes", None, "rows", None), P(None, "rows", None), P(None, "modes"))
    return jax.shard_map(shards, mesh=mesh, in_specs=in_specs, out_specs=out_specs, check_vma=False)
```

```python
import math

import jax
import jax.numpy as jnp
from jax import lax
from jax.experimental import pallas as pl
from jax.experimental.pallas import tpu as pltpu
from jax.sharding import PartitionSpec as P

N = 384
ROWS = 8
CHIPS = 4
PIECE = N // ROWS
MINE = 2
FIELDS = 512
X_STEPS = (1, 2, 3)
Y_STEPS = (8, 16, 24)
Z_STEP = 4
SMEM = pl.BlockSpec(memory_space=pltpu.SMEM)
VMEM = pl.BlockSpec(memory_space=pltpu.VMEM)
ANY = pl.BlockSpec(memory_space=pl.ANY)
LIMIT = 24 * 1024 * 1024
BF16, F32 = jnp.bfloat16, jnp.float32


def sincos(angle):
    y = angle * 0.5
    z = y * y
    s = -1.0 / 39916800.0
    for c in (1.0 / 362880.0, -1.0 / 5040.0, 1.0 / 120.0, -1.0 / 6.0, 1.0):
        s = s * z + c
    s = s * y
    c = 1.0 / 479001600.0
    for d in (-1.0 / 3628800.0, 1.0 / 40320.0, -1.0 / 720.0, 1.0 / 24.0, -0.5, 1.0):
        c = c * z + d
    return 1.0 - 2.0 * s * s, 2.0 * s * c


def dot(a, b):
    return jnp.dot(a, b, preferred_element_type=F32)


def lanes(i):
    return slice(i * N, (i + 1) * N)


def tables_kernel(row_ref, fields_ref, fore_ref, back_ref, keep_ref, give_ref, one, two):
    for r in range(0, N, 128):
        j = lax.broadcasted_iota(jnp.int32, (128, N), 0) + r
        k = lax.broadcasted_iota(jnp.int32, (128, N), 1)
        jk = (j * k).astype(F32)
        turn = jnp.floor(jk * (1.0 / N) + 0.5)
        cosine, sine = sincos((jk - turn * N) * (2.0 * math.pi / N))
        scale = 1.0 / math.sqrt(N)
        cosine = (cosine * scale).astype(BF16)
        sine = (sine * scale).astype(BF16)
        a, b = pl.ds(r, 128), pl.ds(N + r, 128)
        fore_ref[a, :N] = cosine
        fore_ref[a, N:] = -sine
        fore_ref[b, :N] = sine
        fore_ref[b, N:] = cosine
        back_ref[a, :N] = cosine
        back_ref[a, N:] = sine
        back_ref[b, :N] = -sine
        back_ref[b, N:] = cosine
    for f in range(ROWS * MINE):
        for c in range(2):
            one[f * PIECE : (f + 1) * PIECE, lanes(c)] = fields_ref[f, c]
    for h in range(2):
        two[lanes(h), :] = dot(one[lanes(h), :], fore_ref[...]).astype(BF16)
    for k in range(ROWS):
        out = give_ref if k % 2 else keep_ref
        for f in range(MINE):
            top = pl.multiple_of(((row_ref[0] ^ k) * MINE + f) * PIECE, 16)
            for c in range(2):
                out[k // 2, 2 * f + c] = two[pl.ds(top, PIECE), lanes(c)]


def gate_kernel(row_ref):
    del row_ref


def trig_kernel(row_ref, wave_ref, phase_ref, trig_ref):
    for f in range(MINE):
        wave = wave_ref[row_ref[0] * MINE + f]
        for r in range(0, N, 128):
            cosine, sine = sincos(phase_ref[wave, pl.ds(r, 128), :])
            trig_ref[f, 0, pl.ds(r, 128), :] = cosine
            trig_ref[f, 1, pl.ds(r, 128), :] = sine


def mask_kernel(row_ref, mine_ref, got_ref, mask_ref):
    for k in range(ROWS):
        piece = (got_ref if k % 2 else mine_ref)[k // 2]
        top = pl.multiple_of((row_ref[0] ^ k) * PIECE, 16)
        cosine, sine = sincos(piece.astype(F32))
        mask_ref[0, pl.ds(top, PIECE), :] = cosine
        mask_ref[1, pl.ds(top, PIECE), :] = sine


def spectral(sign, fore_ref, back_ref, trig_ref, one, two):
    for c in range(2):
        one[lanes(c), :] = dot(back_ref[lanes(c), :], two[...]).astype(BF16)
    for f in range(MINE):
        re = one[:N, lanes(f)].astype(F32)
        im = one[N:, lanes(f)].astype(F32)
        cosine, sine = trig_ref[f, 0], sign * trig_ref[f, 1]
        two[:N, lanes(f)] = (cosine * re - sine * im).astype(BF16)
        two[N:, lanes(f)] = (sine * re + cosine * im).astype(BF16)
    for c in range(2):
        d = dot(fore_ref[lanes(c), :], two[...]).astype(BF16)
        for f in range(MINE):
            one[lanes(f), lanes(c)] = d[:, lanes(f)]
    return [dot(one[lanes(f), :], back_ref[...]) for f in range(MINE)]


def block_of(blocks, k):
    if k < 2:
        return blocks[k].at[0]
    return blocks[1 + k // 2].at[pl.ds(k % 2 * 2 * MINE, 2 * MINE)]


def forward_kernel(*refs):
    row_ref, blocks = refs[0], refs[1 : 2 + CHIPS]
    fore_ref, back_ref, trig_ref, space_ref, keep_ref, give_ref, one, two = refs[2 + CHIPS :]
    for k in range(ROWS):
        block = block_of(blocks, k)
        top = pl.multiple_of((row_ref[0] ^ k) * PIECE, 16)
        for f in range(MINE):
            for c in range(2):
                one[pl.ds(f * N + top, PIECE), lanes(c)] = block[2 * f + c]
    for f in range(MINE):
        a = dot(one[lanes(f), :], fore_ref[...]).astype(BF16)
        two[:N, lanes(f)] = a[:, :N]
        two[N:, lanes(f)] = a[:, N:]
    space = spectral(1.0, fore_ref, back_ref, trig_ref, one, two)
    for f in range(MINE):
        space_ref[f] = space[f]
        two[lanes(f), :] = space[f].astype(BF16)
    for k in range(ROWS):
        out = give_ref if k % 2 else keep_ref
        top = pl.multiple_of((row_ref[0] ^ k) * PIECE, 16)
        for f in range(MINE):
            for c in range(2):
                out[k // 2, 2 * f + c] = two[pl.ds(f * N + top, PIECE), lanes(c)]


def total(x):
    return jnp.sum(jnp.sum(x, axis=0, keepdims=True), axis=1, keepdims=True)


def backward_kernel(*refs):
    row_ref, blocks = refs[0], refs[1 : 2 + CHIPS]
    fore_ref, back_ref, trig_ref, space_ref, mask_ref = refs[2 + CHIPS : 7 + CHIPS]
    keep_ref, give_ref, one, two, over = refs[7 + CHIPS :]
    for k in range(ROWS):
        block = block_of(blocks, k)
        top = pl.multiple_of((row_ref[0] ^ k) * PIECE, 16)
        for f in range(MINE):
            for c in range(2):
                two[pl.ds(c * N + top, PIECE), lanes(f)] = block[2 * f + c]
    space = spectral(-1.0, fore_ref, back_ref, trig_ref, one, two)
    cosine, sine = mask_ref[0], mask_ref[1]
    over_re, over_im = 0.0, 0.0
    rows = []
    for f in range(MINE):
        b_re, b_im = space[f][:, :N], space[f][:, N:]
        f_re, f_im = space_ref[f, :, :N], space_ref[f, :, N:]
        g_re = f_re * b_re + f_im * b_im
        g_im = f_im * b_re - f_re * b_im
        c_re = total(g_re * cosine - g_im * sine) * (1.0 / N)
        c_im = total(g_re * sine + g_im * cosine) * (1.0 / N)
        over_re = over_re + (g_re * c_re + g_im * c_im)
        over_im = over_im + (g_im * c_re - g_re * c_im)
        rows += [c_re, c_im]
    scale = 1.0 / math.sqrt(FIELDS)
    over[0] = (over_re * scale).astype(BF16)
    over[1] = (over_im * scale).astype(BF16)
    for k in range(ROWS):
        out = give_ref if k % 2 else keep_ref
        top = pl.multiple_of((row_ref[0] ^ k) * PIECE, 16)
        for c in range(2):
            start = ((k // 2) * 2 + c) * PIECE
            out[start : start + PIECE, :] = over[c, pl.ds(top, PIECE), :]
    high = [r.astype(BF16) for r in rows]
    rest = [r - h.astype(F32) for r, h in zip(rows, high)]
    mid = [r.astype(BF16) for r in rest]
    low = [(r - m.astype(F32)).astype(BF16) for r, m in zip(rest, mid)]
    at = lax.broadcasted_iota(jnp.int32, (16, N), 0)
    packed = jnp.zeros((16, N), F32)
    for t, terms in enumerate((high, mid, low)):
        for i, value in enumerate(terms):
            packed = jnp.where(at == 4 * t + i, value.astype(F32), packed)
    for out in (keep_ref, give_ref):
        out[CHIPS * 2 * PIECE :, :] = packed.astype(BF16)


def core_sum_kernel(keep_ref, got_ref, *outs):
    tail = CHIPS * 2 * PIECE
    for j in range(CHIPS):
        at = slice(j * 2 * PIECE, (j + 1) * 2 * PIECE)
        both = keep_ref[at, :].astype(F32) + got_ref[at, :].astype(F32)
        outs[j][: 2 * PIECE, :] = both.astype(BF16)
        outs[j][2 * PIECE :, :128] = keep_ref[tail:, :128]
        outs[j][2 * PIECE :, 128:256] = got_ref[tail:, 128:256]
        outs[j][2 * PIECE :, 256:] = keep_ref[tail:, 256:]


def four(terms):
    terms = [t.astype(F32) for t in terms]
    return (terms[0] + terms[1]) + (terms[2] + terms[3])


def chip_sum_kernel(at_ref, *refs):
    parts, (over_ref, coup_ref) = refs[:CHIPS], refs[-2:]
    over_ref[...] = four([p[: 2 * PIECE, :] for p in parts]).astype(BF16)
    at = lax.broadcasted_iota(jnp.int32, (1, 128), 1)
    result = [jnp.zeros((1, 128), F32)] * 2
    for k in range(ROWS):
        half = slice(128 * (k % 2), 128 * (k % 2) + 128)
        packed = parts[k // 2][2 * PIECE :, half].astype(F32)
        for f in range(MINE):
            here = at == (at_ref[0] ^ k) * MINE + f
            for c in range(2):
                i = 2 * f + c
                value = packed[i : i + 1] + packed[4 + i : 5 + i] + packed[8 + i : 9 + i]
                result[c] = jnp.where(here, value, result[c])
    coup_ref[...] = jnp.concatenate(result, axis=0)[:, : ROWS * MINE]


def four_sum_kernel(*refs):
    refs[-1][...] = four([r[...] for r in refs[:4]]).astype(BF16)


def final_kernel(row_ref, *refs):
    over_ref, more_ref, *blocks, out_ref, mask_ref = refs
    over = over_ref[...].astype(F32) + more_ref[...].astype(F32)
    re, im = over[:PIECE], over[PIECE:]
    denom = jnp.maximum(jnp.sqrt(re * re + im * im), 1.0)
    re, im = re / denom, im / denom
    mask_ref[0] = re
    mask_ref[1] = im
    for k in range(ROWS):
        block = block_of(blocks, k)
        first = (row_ref[0] ^ k) * MINE
        for f in range(MINE):
            f_re = block[2 * f].astype(F32)
            f_im = block[2 * f + 1].astype(F32)
            out_ref[first + f, 0] = (f_re * re - f_im * im).astype(BF16)
            out_ref[first + f, 1] = (f_re * im + f_im * re).astype(BF16)


def cut_kernel(row_ref, fields_ref, keep_ref, give_ref, sems):
    copies = []
    for k in range(ROWS):
        out = (give_ref if k % 2 else keep_ref).at[k // 2]
        mine = fields_ref.at[pl.ds((row_ref[0] ^ k) * 2 * MINE, 2 * MINE)]
        copies.append(pltpu.make_async_copy(mine, out, sems.at[k]))
    for copy in copies:
        copy.start()
    for copy in copies:
        copy.wait()


def call(kernel, args, outs, scratch=(), flops=0, after=(), places=None, sems=0, through=()):
    args, after = list(args), list(after) + list(through)
    first = len(args) + len(after) - len(through)
    alias = {first + i: len(outs) + i for i in range(len(through))}
    size = sum(a.size * a.dtype.itemsize for a in args) + sum(
        math.prod(s) * jnp.dtype(t).itemsize for s, t in outs
    )
    place = places or VMEM
    scratch_shapes = [pltpu.VMEM(s, t) for s, t in scratch]
    n, m = len(args), len(args) + len(after) + len(outs)

    def body(*refs):
        kernel(*refs[:n], *refs[n + len(after) : m], *refs[m + len(through) :])

    outputs = pl.pallas_call(
        body,
        name=kernel.__name__,
        out_shape=[jax.ShapeDtypeStruct(s, t) for s, t in outs]
        + [jax.ShapeDtypeStruct(t.shape, t.dtype) for t in through],
        in_specs=[SMEM if a.dtype == jnp.int32 else place for a in args] + [ANY] * len(after),
        out_specs=[place] * len(outs) + [ANY] * len(through),
        input_output_aliases=alias,
        scratch_shapes=scratch_shapes + [pltpu.SemaphoreType.DMA((sems,))] * (sems > 0),
        compiler_params=pltpu.CompilerParams(vmem_limit_bytes=LIMIT),
        cost_estimate=pl.CostEstimate(flops=flops, bytes_accessed=size, transcendentals=0),
    )(*args, *after)
    return list(outputs)


def over_rows(block, k, name):
    with jax.named_scope(name):
        return lax.ppermute(block, "rows", [(s, s ^ k) for s in range(ROWS)])


def over_modes(block, k, name):
    with jax.named_scope(name):
        return lax.ppermute(block, "modes", [(s, s ^ k) for s in range(lax.axis_size("modes"))])


def both_cores(keep, give, name, more=()):
    got = over_rows(give, 1, name)
    pairs = [jnp.concatenate([keep[j], got[j], *more]) for j in range(1, CHIPS)]
    return keep, got, pairs


def shards(fwd_fields, bwd_fields, wavelength, kernel_phase, mask_phase):
    at = lax.axis_index("rows").astype(jnp.int32)[None]

    sent = ((CHIPS, 2 * MINE, PIECE, N), BF16)
    low_mask = mask_phase.astype(BF16)[None]
    keep, give = call(
        cut_kernel, [at, fwd_fields.reshape(-1, PIECE, N)], [sent] * 2, places=pl.BlockSpec(memory_space=pltpu.HBM), sems=ROWS
    )
    keep, got, pairs = both_cores(keep, give, "forward_entry_core", [low_mask])
    fwd_blocks = [keep, got] + [
        over_rows(p, 2 * j + 2, f"forward_entry_chip{j + 1}") for j, p in enumerate(pairs)
    ]
    masks = jnp.concatenate([low_mask] + [b[4 * MINE :] for b in fwd_blocks[2:]])
    (mask,) = call(
        mask_kernel, [at, masks, over_rows(masks, 1, "mask_core")], [((2, N, N), F32)]
    )

    wide = (2 * N, 2 * N)
    scratch = [(wide, BF16), (wide, BF16)]
    work = 2 * (2 * N) ** 3
    fore, back, keep, give = call(
        tables_kernel, [at, bwd_fields], [(wide, BF16), (wide, BF16), sent, sent], scratch, work
    )
    got = over_rows(give, 1, "backward_entry_core")
    trig, got = call(
        trig_kernel,
        [at, wavelength, kernel_phase],
        [((MINE, 2, N, N), F32)],
        after=fwd_blocks[2:3],
        through=[got],
    )
    (got,) = call(gate_kernel, [at], [], after=fwd_blocks[3:4], through=[got])
    pairs = [jnp.concatenate([keep[j], got[j]]) for j in range(1, CHIPS)]
    bwd_blocks = [keep, got] + [
        over_rows(p, 2 * j + 2, f"backward_entry_chip{j + 1}") for j, p in enumerate(pairs)
    ]

    space, keep, give = call(
        forward_kernel,
        [at, *fwd_blocks, fore, back, trig],
        [((MINE, N, 2 * N), F32), sent, sent],
        scratch,
        4 * work,
    )
    keep, got, pairs = both_cores(keep, give, "forward_exit_core")
    size = CHIPS * 2 * PIECE + 16
    over_keep, over_give = call(
        backward_kernel,
        [at, *bwd_blocks, fore, back, trig, space, mask],
        [((size, N), BF16), ((size, N), BF16)],
        scratch + [((2, N, N), BF16)],
        3 * work,
    )
    over_got = over_rows(over_give, 1, "over_core")
    sums = call(
        core_sum_kernel,
        [over_keep, over_got],
        [((2 * PIECE + 16, N), BF16)] * CHIPS,
        after=[got],
    )
    parts = [sums[0]] + [over_rows(sums[j], 2 * j, f"over_chip{j}") for j in range(1, CHIPS)]
    small = ((2 * PIECE, N), BF16)
    over, coupling, *pairs = call(
        chip_sum_kernel, [at, *parts], [small, ((2, ROWS * MINE), F32)], through=pairs
    )
    near, far, last = [
        over_rows(p, 2 * j + 2, f"forward_exit_chip{j + 1}") for j, p in enumerate(pairs)
    ]
    terms = [over] + [over_modes(over, k, f"over_x{k}") for k in X_STEPS]
    (over,) = call(four_sum_kernel, terms, [small])
    terms = [over] + [over_modes(over, k, f"over_y{k // 8}") for k in Y_STEPS]
    (over,) = call(four_sum_kernel, terms, [small], after=[far])
    fwd_out, new_mask = call(
        final_kernel,
        [at, over, over_modes(over, Z_STEP, "over_z"), keep, got, near, far, last],
        [((ROWS * MINE, 2, PIECE, N), BF16), ((2, PIECE, N), F32)],
    )
    return fwd_out, new_mask, coupling


def solution(mesh):
    in_specs = (
        P("modes", None, "rows", None),
        P("modes", None, "rows", None),
        P("modes"),
        P(),
        P("rows", None),
    )
    out_specs = (P("modes", None, "rows", None), P(None, "rows", None), P(None, "modes"))
    return jax.shard_map(shards, mesh=mesh, in_specs=in_specs, out_specs=out_specs, check_vma=False)
```

```python
import math

import jax
import jax.numpy as jnp
from jax import lax
from jax.experimental import pallas as pl
from jax.experimental.pallas import tpu as pltpu
from jax.sharding import PartitionSpec as P

N = 384
ROWS = 8
CHIPS = 4
PIECE = N // ROWS
MINE = 2
FIELDS = 512
X_STEPS = (1, 2, 3)
Y_STEPS = (8, 16, 24)
Z_STEP = 4
SMEM = pl.BlockSpec(memory_space=pltpu.SMEM)
VMEM = pl.BlockSpec(memory_space=pltpu.VMEM)
ANY = pl.BlockSpec(memory_space=pl.ANY)
LIMIT = 24 * 1024 * 1024
BF16, F32 = jnp.bfloat16, jnp.float32


def sincos(angle):
    y = angle * 0.5
    z = y * y
    s = -1.0 / 39916800.0
    for c in (1.0 / 362880.0, -1.0 / 5040.0, 1.0 / 120.0, -1.0 / 6.0, 1.0):
        s = s * z + c
    s = s * y
    c = 1.0 / 479001600.0
    for d in (-1.0 / 3628800.0, 1.0 / 40320.0, -1.0 / 720.0, 1.0 / 24.0, -0.5, 1.0):
        c = c * z + d
    return 1.0 - 2.0 * s * s, 2.0 * s * c


def dot(a, b):
    return jnp.dot(a, b, preferred_element_type=F32)


def lanes(i):
    return slice(i * N, (i + 1) * N)


def tables_kernel(row_ref, fields_ref, fore_ref, back_ref, keep_ref, give_ref, one, two):
    for r in range(0, N, 128):
        j = lax.broadcasted_iota(jnp.int32, (128, N), 0) + r
        k = lax.broadcasted_iota(jnp.int32, (128, N), 1)
        jk = (j * k).astype(F32)
        turn = jnp.floor(jk * (1.0 / N) + 0.5)
        cosine, sine = sincos((jk - turn * N) * (2.0 * math.pi / N))
        scale = 1.0 / math.sqrt(N)
        cosine = (cosine * scale).astype(BF16)
        sine = (sine * scale).astype(BF16)
        a, b = pl.ds(r, 128), pl.ds(N + r, 128)
        fore_ref[a, :N] = cosine
        fore_ref[a, N:] = -sine
        fore_ref[b, :N] = sine
        fore_ref[b, N:] = cosine
        back_ref[a, :N] = cosine
        back_ref[a, N:] = sine
        back_ref[b, :N] = -sine
        back_ref[b, N:] = cosine
    for f in range(ROWS * MINE):
        for c in range(2):
            one[f * PIECE : (f + 1) * PIECE, lanes(c)] = fields_ref[f, c]
    for h in range(2):
        two[lanes(h), :] = dot(one[lanes(h), :], fore_ref[...]).astype(BF16)
    for k in range(ROWS):
        out = give_ref if k % 2 else keep_ref
        for f in range(MINE):
            top = pl.multiple_of(((row_ref[0] ^ k) * MINE + f) * PIECE, 16)
            for c in range(2):
                out[k // 2, 2 * f + c] = two[pl.ds(top, PIECE), lanes(c)]


def gate_kernel(row_ref):
    del row_ref


def trig_kernel(row_ref, wave_ref, phase_ref, trig_ref):
    for f in range(MINE):
        wave = wave_ref[row_ref[0] * MINE + f]
        for r in range(0, N, 128):
            cosine, sine = sincos(phase_ref[wave, pl.ds(r, 128), :])
            trig_ref[f, 0, pl.ds(r, 128), :] = cosine
            trig_ref[f, 1, pl.ds(r, 128), :] = sine


def mask_kernel(row_ref, mine_ref, got_ref, mask_ref):
    for k in range(ROWS):
        piece = (got_ref if k % 2 else mine_ref)[k // 2]
        top = pl.multiple_of((row_ref[0] ^ k) * PIECE, 16)
        cosine, sine = sincos(piece.astype(F32))
        mask_ref[0, pl.ds(top, PIECE), :] = cosine
        mask_ref[1, pl.ds(top, PIECE), :] = sine


def spectral(sign, fore_ref, back_ref, trig_ref, one, two):
    for c in range(2):
        one[lanes(c), :] = dot(back_ref[lanes(c), :], two[...]).astype(BF16)
    for f in range(MINE):
        re = one[:N, lanes(f)].astype(F32)
        im = one[N:, lanes(f)].astype(F32)
        cosine, sine = trig_ref[f, 0], sign * trig_ref[f, 1]
        two[:N, lanes(f)] = (cosine * re - sine * im).astype(BF16)
        two[N:, lanes(f)] = (sine * re + cosine * im).astype(BF16)
    for c in range(2):
        d = dot(fore_ref[lanes(c), :], two[...]).astype(BF16)
        for f in range(MINE):
            one[lanes(f), lanes(c)] = d[:, lanes(f)]
    return [dot(one[lanes(f), :], back_ref[...]) for f in range(MINE)]


def block_of(blocks, k):
    if k < 2:
        return blocks[k].at[0]
    return blocks[1 + k // 2].at[pl.ds(k % 2 * 2 * MINE, 2 * MINE)]


def forward_kernel(*refs):
    row_ref, blocks = refs[0], refs[1 : 2 + CHIPS]
    fore_ref, back_ref, trig_ref, space_ref, keep_ref, give_ref, one, two = refs[2 + CHIPS :]
    for k in range(ROWS):
        block = block_of(blocks, k)
        top = pl.multiple_of((row_ref[0] ^ k) * PIECE, 16)
        for f in range(MINE):
            for c in range(2):
                one[pl.ds(f * N + top, PIECE), lanes(c)] = block[2 * f + c]
    for f in range(MINE):
        a = dot(one[lanes(f), :], fore_ref[...]).astype(BF16)
        two[:N, lanes(f)] = a[:, :N]
        two[N:, lanes(f)] = a[:, N:]
    space = spectral(1.0, fore_ref, back_ref, trig_ref, one, two)
    for f in range(MINE):
        space_ref[f] = space[f]
        two[lanes(f), :] = space[f].astype(BF16)
    for k in range(ROWS):
        out = give_ref if k % 2 else keep_ref
        top = pl.multiple_of((row_ref[0] ^ k) * PIECE, 16)
        for f in range(MINE):
            for c in range(2):
                out[k // 2, 2 * f + c] = two[pl.ds(f * N + top, PIECE), lanes(c)]


def total(x):
    return jnp.sum(jnp.sum(x, axis=0, keepdims=True), axis=1, keepdims=True)


def backward_kernel(*refs):
    row_ref, blocks = refs[0], refs[1 : 2 + CHIPS]
    fore_ref, back_ref, trig_ref, space_ref, mask_ref = refs[2 + CHIPS : 7 + CHIPS]
    keep_ref, give_ref, one, two, over = refs[7 + CHIPS :]
    for k in range(ROWS):
        block = block_of(blocks, k)
        top = pl.multiple_of((row_ref[0] ^ k) * PIECE, 16)
        for f in range(MINE):
            for c in range(2):
                two[pl.ds(c * N + top, PIECE), lanes(f)] = block[2 * f + c]
    space = spectral(-1.0, fore_ref, back_ref, trig_ref, one, two)
    cosine, sine = mask_ref[0], mask_ref[1]
    over_re, over_im = 0.0, 0.0
    rows = []
    for f in range(MINE):
        b_re, b_im = space[f][:, :N], space[f][:, N:]
        f_re, f_im = space_ref[f, :, :N], space_ref[f, :, N:]
        g_re = f_re * b_re + f_im * b_im
        g_im = f_im * b_re - f_re * b_im
        c_re = total(g_re * cosine - g_im * sine) * (1.0 / N)
        c_im = total(g_re * sine + g_im * cosine) * (1.0 / N)
        over_re = over_re + (g_re * c_re + g_im * c_im)
        over_im = over_im + (g_im * c_re - g_re * c_im)
        rows += [c_re, c_im]
    scale = 1.0 / math.sqrt(FIELDS)
    over[0] = (over_re * scale).astype(BF16)
    over[1] = (over_im * scale).astype(BF16)
    for k in range(ROWS):
        out = give_ref if k % 2 else keep_ref
        top = pl.multiple_of((row_ref[0] ^ k) * PIECE, 16)
        for c in range(2):
            start = ((k // 2) * 2 + c) * PIECE
            out[start : start + PIECE, :] = over[c, pl.ds(top, PIECE), :]
    high = [r.astype(BF16) for r in rows]
    rest = [r - h.astype(F32) for r, h in zip(rows, high)]
    mid = [r.astype(BF16) for r in rest]
    low = [(r - m.astype(F32)).astype(BF16) for r, m in zip(rest, mid)]
    at = lax.broadcasted_iota(jnp.int32, (16, N), 0)
    packed = jnp.zeros((16, N), F32)
    for t, terms in enumerate((high, mid, low)):
        for i, value in enumerate(terms):
            packed = jnp.where(at == 4 * t + i, value.astype(F32), packed)
    for out in (keep_ref, give_ref):
        out[CHIPS * 2 * PIECE :, :] = packed.astype(BF16)


def core_sum_kernel(keep_ref, got_ref, *outs):
    tail = CHIPS * 2 * PIECE
    for j in range(CHIPS):
        at = slice(j * 2 * PIECE, (j + 1) * 2 * PIECE)
        both = keep_ref[at, :].astype(F32) + got_ref[at, :].astype(F32)
        outs[j][: 2 * PIECE, :] = both.astype(BF16)
        outs[j][2 * PIECE :, :128] = keep_ref[tail:, :128]
        outs[j][2 * PIECE :, 128:256] = got_ref[tail:, 128:256]
        outs[j][2 * PIECE :, 256:] = keep_ref[tail:, 256:]


def four(terms):
    terms = [t.astype(F32) for t in terms]
    return (terms[0] + terms[1]) + (terms[2] + terms[3])


def chip_sum_kernel(at_ref, *refs):
    parts, (over_ref, coup_ref) = refs[:CHIPS], refs[-2:]
    over_ref[...] = four([p[: 2 * PIECE, :] for p in parts]).astype(BF16)
    at = lax.broadcasted_iota(jnp.int32, (1, 128), 1)
    result = [jnp.zeros((1, 128), F32)] * 2
    for k in range(ROWS):
        half = slice(128 * (k % 2), 128 * (k % 2) + 128)
        packed = parts[k // 2][2 * PIECE :, half].astype(F32)
        for f in range(MINE):
            here = at == (at_ref[0] ^ k) * MINE + f
            for c in range(2):
                i = 2 * f + c
                value = packed[i : i + 1] + packed[4 + i : 5 + i] + packed[8 + i : 9 + i]
                result[c] = jnp.where(here, value, result[c])
    coup_ref[...] = jnp.concatenate(result, axis=0)[:, : ROWS * MINE]


def four_sum_kernel(*refs):
    refs[-1][...] = four([r[...] for r in refs[:4]]).astype(BF16)


def final_kernel(row_ref, *refs):
    over_ref, more_ref, *blocks, out_ref, mask_ref = refs
    over = over_ref[...].astype(F32) + more_ref[...].astype(F32)
    re, im = over[:PIECE], over[PIECE:]
    denom = jnp.maximum(jnp.sqrt(re * re + im * im), 1.0)
    re, im = re / denom, im / denom
    mask_ref[0] = re
    mask_ref[1] = im
    for k in range(ROWS):
        block = block_of(blocks, k)
        first = (row_ref[0] ^ k) * MINE
        for f in range(MINE):
            f_re = block[2 * f].astype(F32)
            f_im = block[2 * f + 1].astype(F32)
            out_ref[first + f, 0] = (f_re * re - f_im * im).astype(BF16)
            out_ref[first + f, 1] = (f_re * im + f_im * re).astype(BF16)


def cut_kernel(row_ref, fields_ref, keep_ref, give_ref):
    for k in range(ROWS):
        out = give_ref if k % 2 else keep_ref
        out[k // 2] = fields_ref[pl.ds((row_ref[0] ^ k) * 2 * MINE, 2 * MINE)]


def call(kernel, args, outs, scratch=(), flops=0, after=(), through=()):
    args, after = list(args), list(after) + list(through)
    first = len(args) + len(after) - len(through)
    alias = {first + i: len(outs) + i for i in range(len(through))}
    size = sum(a.size * a.dtype.itemsize for a in args) + sum(
        math.prod(s) * jnp.dtype(t).itemsize for s, t in outs
    )
    n, m = len(args), len(args) + len(after) + len(outs)

    def body(*refs):
        kernel(*refs[:n], *refs[n + len(after) : m], *refs[m + len(through) :])

    outputs = pl.pallas_call(
        body,
        name=kernel.__name__,
        out_shape=[jax.ShapeDtypeStruct(s, t) for s, t in outs]
        + [jax.ShapeDtypeStruct(t.shape, t.dtype) for t in through],
        in_specs=[SMEM if a.dtype == jnp.int32 else VMEM for a in args] + [ANY] * len(after),
        out_specs=[VMEM] * len(outs) + [ANY] * len(through),
        input_output_aliases=alias,
        scratch_shapes=[pltpu.VMEM(s, t) for s, t in scratch],
        compiler_params=pltpu.CompilerParams(vmem_limit_bytes=LIMIT),
        cost_estimate=pl.CostEstimate(flops=flops, bytes_accessed=size, transcendentals=0),
    )(*args, *after)
    return list(outputs)


def over_rows(block, k, name):
    with jax.named_scope(name):
        return lax.ppermute(block, "rows", [(s, s ^ k) for s in range(ROWS)])


def over_modes(block, k, name):
    with jax.named_scope(name):
        return lax.ppermute(block, "modes", [(s, s ^ k) for s in range(lax.axis_size("modes"))])


def both_cores(keep, give, name, more=()):
    got = over_rows(give, 1, name)
    pairs = [jnp.concatenate([keep[j], got[j], *more]) for j in range(1, CHIPS)]
    return keep, got, pairs


def shards(fwd_fields, bwd_fields, wavelength, kernel_phase, mask_phase):
    at = lax.axis_index("rows").astype(jnp.int32)[None]

    sent = ((CHIPS, 2 * MINE, PIECE, N), BF16)
    low_mask = mask_phase.astype(BF16)[None]
    keep, give = call(cut_kernel, [at, fwd_fields.reshape(-1, PIECE, N)], [sent] * 2)
    keep, got, pairs = both_cores(keep, give, "forward_entry_core", [low_mask])
    fwd_blocks = [keep, got] + [
        over_rows(p, 2 * j + 2, f"forward_entry_chip{j + 1}") for j, p in enumerate(pairs)
    ]
    masks = jnp.concatenate([low_mask] + [b[4 * MINE :] for b in fwd_blocks[2:]])
    (mask,) = call(
        mask_kernel, [at, masks, over_rows(masks, 1, "mask_core")], [((2, N, N), F32)]
    )

    wide = (2 * N, 2 * N)
    scratch = [(wide, BF16), (wide, BF16)]
    work = 2 * (2 * N) ** 3
    fore, back, keep, give = call(
        tables_kernel, [at, bwd_fields], [(wide, BF16), (wide, BF16), sent, sent], scratch, work
    )
    got = over_rows(give, 1, "backward_entry_core")
    trig, got = call(
        trig_kernel,
        [at, wavelength, kernel_phase],
        [((MINE, 2, N, N), F32)],
        after=fwd_blocks[2:3],
        through=[got],
    )
    (got,) = call(gate_kernel, [at], [], after=fwd_blocks[3:4], through=[got])
    pairs = [jnp.concatenate([keep[j], got[j]]) for j in range(1, CHIPS)]
    bwd_blocks = [keep, got] + [
        over_rows(p, 2 * j + 2, f"backward_entry_chip{j + 1}") for j, p in enumerate(pairs)
    ]

    space, keep, give = call(
        forward_kernel,
        [at, *fwd_blocks, fore, back, trig],
        [((MINE, N, 2 * N), F32), sent, sent],
        scratch,
        4 * work,
    )
    keep, got, pairs = both_cores(keep, give, "forward_exit_core")
    start1, pairs[1] = over_rows(keep[2], 4, "forward_exit_start2"), got[2]
    size = CHIPS * 2 * PIECE + 16
    over_keep, over_give = call(
        backward_kernel,
        [at, *bwd_blocks, fore, back, trig, space, mask],
        [((size, N), BF16), ((size, N), BF16)],
        scratch + [((2, N, N), BF16)],
        3 * work,
    )
    over_got = over_rows(over_give, 1, "over_core")
    sums = call(
        core_sum_kernel,
        [over_keep, over_got],
        [((2 * PIECE + 16, N), BF16)] * CHIPS,
        after=[got],
    )
    parts = [sums[0]] + [over_rows(sums[j], 2 * j, f"over_chip{j}") for j in range(1, CHIPS)]
    small = ((2 * PIECE, N), BF16)
    over, coupling, *pairs = call(
        chip_sum_kernel,
        [at, *parts],
        [small, ((2, ROWS * MINE), F32)],
        after=[start1],
        through=pairs,

    )
    near, far, last = [
        over_rows(p, 2 * j + 2, f"forward_exit_chip{j + 1}") for j, p in enumerate(pairs)
    ]
    far = jnp.concatenate([start1, far])
    terms = [over] + [over_modes(over, k, f"over_x{k}") for k in X_STEPS]
    (over,) = call(four_sum_kernel, terms, [small])
    terms = [over] + [over_modes(over, k, f"over_y{k // 8}") for k in Y_STEPS]
    (over,) = call(four_sum_kernel, terms, [small], after=[far])
    fwd_out, new_mask = call(
        final_kernel,
        [at, over, over_modes(over, Z_STEP, "over_z"), keep, got, near, far, last],
        [((ROWS * MINE, 2, PIECE, N), BF16), ((2, PIECE, N), F32)],
    )
    return fwd_out, new_mask, coupling


def solution(mesh):
    in_specs = (
        P("modes", None, "rows", None),
        P("modes", None, "rows", None),
        P("modes"),
        P(),
        P("rows", None),
    )
    out_specs = (P("modes", None, "rows", None), P(None, "rows", None), P(None, "modes"))
    return jax.shard_map(shards, mesh=mesh, in_specs=in_specs, out_specs=out_specs, check_vma=False)
```

```python
import math

import jax
import jax.numpy as jnp
from jax import lax
from jax.experimental import pallas as pl
from jax.experimental.pallas import tpu as pltpu
from jax.sharding import PartitionSpec as P

N = 384
ROWS = 8
CHIPS = 4
PIECE = N // ROWS
MINE = 2
FIELDS = 512
X_STEPS = (1, 2, 3)
Y_STEPS = (8, 16, 24)
Z_STEP = 4
SMEM = pl.BlockSpec(memory_space=pltpu.SMEM)
VMEM = pl.BlockSpec(memory_space=pltpu.VMEM)
ANY = pl.BlockSpec(memory_space=pl.ANY)
LIMIT = 24 * 1024 * 1024
BF16, F32 = jnp.bfloat16, jnp.float32


def sincos(angle):
    y = angle * 0.5
    z = y * y
    s = -1.0 / 39916800.0
    for c in (1.0 / 362880.0, -1.0 / 5040.0, 1.0 / 120.0, -1.0 / 6.0, 1.0):
        s = s * z + c
    s = s * y
    c = 1.0 / 479001600.0
    for d in (-1.0 / 3628800.0, 1.0 / 40320.0, -1.0 / 720.0, 1.0 / 24.0, -0.5, 1.0):
        c = c * z + d
    return 1.0 - 2.0 * s * s, 2.0 * s * c


def dot(a, b):
    return jnp.dot(a, b, preferred_element_type=F32)


def lanes(i):
    return slice(i * N, (i + 1) * N)


def tables_kernel(row_ref, fields_ref, fore_ref, back_ref, keep_ref, give_ref, one, two):
    for r in range(0, N, 128):
        j = lax.broadcasted_iota(jnp.int32, (128, N), 0) + r
        k = lax.broadcasted_iota(jnp.int32, (128, N), 1)
        jk = (j * k).astype(F32)
        turn = jnp.floor(jk * (1.0 / N) + 0.5)
        cosine, sine = sincos((jk - turn * N) * (2.0 * math.pi / N))
        scale = 1.0 / math.sqrt(N)
        cosine = (cosine * scale).astype(BF16)
        sine = (sine * scale).astype(BF16)
        a, b = pl.ds(r, 128), pl.ds(N + r, 128)
        fore_ref[a, :N] = cosine
        fore_ref[a, N:] = -sine
        fore_ref[b, :N] = sine
        fore_ref[b, N:] = cosine
        back_ref[a, :N] = cosine
        back_ref[a, N:] = sine
        back_ref[b, :N] = -sine
        back_ref[b, N:] = cosine
    for f in range(ROWS * MINE):
        for c in range(2):
            one[f * PIECE : (f + 1) * PIECE, lanes(c)] = fields_ref[f, c]
    for h in range(2):
        two[lanes(h), :] = dot(one[lanes(h), :], fore_ref[...]).astype(BF16)
    for k in range(ROWS):
        out = give_ref if k % 2 else keep_ref
        for f in range(MINE):
            top = pl.multiple_of(((row_ref[0] ^ k) * MINE + f) * PIECE, 16)
            for c in range(2):
                out[k // 2, 2 * f + c] = two[pl.ds(top, PIECE), lanes(c)]


def gate_kernel(row_ref):
    del row_ref


def trig_kernel(row_ref, wave_ref, phase_ref, trig_ref):
    for f in range(MINE):
        wave = wave_ref[row_ref[0] * MINE + f]
        for r in range(0, N, 128):
            cosine, sine = sincos(phase_ref[wave, pl.ds(r, 128), :])
            trig_ref[f, 0, pl.ds(r, 128), :] = cosine
            trig_ref[f, 1, pl.ds(r, 128), :] = sine


def mask_kernel(row_ref, mine_ref, got_ref, mask_ref):
    for k in range(ROWS):
        piece = (got_ref if k % 2 else mine_ref)[k // 2]
        top = pl.multiple_of((row_ref[0] ^ k) * PIECE, 16)
        cosine, sine = sincos(piece.astype(F32))
        mask_ref[0, pl.ds(top, PIECE), :] = cosine
        mask_ref[1, pl.ds(top, PIECE), :] = sine


def spectral(sign, fore_ref, back_ref, trig_ref, one, two):
    for c in range(2):
        one[lanes(c), :] = dot(back_ref[lanes(c), :], two[...]).astype(BF16)
    for f in range(MINE):
        re = one[:N, lanes(f)].astype(F32)
        im = one[N:, lanes(f)].astype(F32)
        cosine, sine = trig_ref[f, 0], sign * trig_ref[f, 1]
        two[:N, lanes(f)] = (cosine * re - sine * im).astype(BF16)
        two[N:, lanes(f)] = (sine * re + cosine * im).astype(BF16)
    for c in range(2):
        d = dot(fore_ref[lanes(c), :], two[...]).astype(BF16)
        for f in range(MINE):
            one[lanes(f), lanes(c)] = d[:, lanes(f)]
    return [dot(one[lanes(f), :], back_ref[...]) for f in range(MINE)]


def block_of(blocks, k):
    if k < 2:
        return blocks[k].at[0]
    return blocks[1 + k // 2].at[pl.ds(k % 2 * 2 * MINE, 2 * MINE)]


def forward_kernel(*refs):
    row_ref, blocks = refs[0], refs[1 : 2 + CHIPS]
    fore_ref, back_ref, trig_ref, space_ref, keep_ref, give_ref, one, two = refs[2 + CHIPS :]
    for k in range(ROWS):
        block = block_of(blocks, k)
        top = pl.multiple_of((row_ref[0] ^ k) * PIECE, 16)
        for f in range(MINE):
            for c in range(2):
                one[pl.ds(f * N + top, PIECE), lanes(c)] = block[2 * f + c]
    for f in range(MINE):
        a = dot(one[lanes(f), :], fore_ref[...]).astype(BF16)
        two[:N, lanes(f)] = a[:, :N]
        two[N:, lanes(f)] = a[:, N:]
    space = spectral(1.0, fore_ref, back_ref, trig_ref, one, two)
    for f in range(MINE):
        space_ref[f] = space[f]
        two[lanes(f), :] = space[f].astype(BF16)
    for k in range(ROWS):
        out = give_ref if k % 2 else keep_ref
        top = pl.multiple_of((row_ref[0] ^ k) * PIECE, 16)
        for f in range(MINE):
            for c in range(2):
                out[k // 2, 2 * f + c] = two[pl.ds(f * N + top, PIECE), lanes(c)]


def total(x):
    return jnp.sum(jnp.sum(x, axis=0, keepdims=True), axis=1, keepdims=True)


def backward_kernel(*refs):
    row_ref, blocks = refs[0], refs[1 : 2 + CHIPS]
    fore_ref, back_ref, trig_ref, space_ref, mask_ref = refs[2 + CHIPS : 7 + CHIPS]
    keep_ref, give_ref, one, two, over = refs[7 + CHIPS :]
    for k in range(ROWS):
        block = block_of(blocks, k)
        top = pl.multiple_of((row_ref[0] ^ k) * PIECE, 16)
        for f in range(MINE):
            for c in range(2):
                two[pl.ds(c * N + top, PIECE), lanes(f)] = block[2 * f + c]
    space = spectral(-1.0, fore_ref, back_ref, trig_ref, one, two)
    cosine, sine = mask_ref[0], mask_ref[1]
    over_re, over_im = 0.0, 0.0
    rows = []
    for f in range(MINE):
        b_re, b_im = space[f][:, :N], space[f][:, N:]
        f_re, f_im = space_ref[f, :, :N], space_ref[f, :, N:]
        g_re = f_re * b_re + f_im * b_im
        g_im = f_im * b_re - f_re * b_im
        c_re = total(g_re * cosine - g_im * sine) * (1.0 / N)
        c_im = total(g_re * sine + g_im * cosine) * (1.0 / N)
        over_re = over_re + (g_re * c_re + g_im * c_im)
        over_im = over_im + (g_im * c_re - g_re * c_im)
        rows += [c_re, c_im]
    scale = 1.0 / math.sqrt(FIELDS)
    over[0] = (over_re * scale).astype(BF16)
    over[1] = (over_im * scale).astype(BF16)
    for k in range(ROWS):
        out = give_ref if k % 2 else keep_ref
        top = pl.multiple_of((row_ref[0] ^ k) * PIECE, 16)
        for c in range(2):
            start = ((k // 2) * 2 + c) * PIECE
            out[start : start + PIECE, :] = over[c, pl.ds(top, PIECE), :]
    high = [r.astype(BF16) for r in rows]
    rest = [r - h.astype(F32) for r, h in zip(rows, high)]
    mid = [r.astype(BF16) for r in rest]
    low = [(r - m.astype(F32)).astype(BF16) for r, m in zip(rest, mid)]
    at = lax.broadcasted_iota(jnp.int32, (16, N), 0)
    packed = jnp.zeros((16, N), F32)
    for t, terms in enumerate((high, mid, low)):
        for i, value in enumerate(terms):
            packed = jnp.where(at == 4 * t + i, value.astype(F32), packed)
    for out in (keep_ref, give_ref):
        out[CHIPS * 2 * PIECE :, :] = packed.astype(BF16)


def core_sum_kernel(keep_ref, got_ref, *outs):
    tail = CHIPS * 2 * PIECE
    for j in range(CHIPS):
        at = slice(j * 2 * PIECE, (j + 1) * 2 * PIECE)
        both = keep_ref[at, :].astype(F32) + got_ref[at, :].astype(F32)
        outs[j][: 2 * PIECE, :] = both.astype(BF16)
        outs[j][2 * PIECE :, :128] = keep_ref[tail:, :128]
        outs[j][2 * PIECE :, 128:256] = got_ref[tail:, 128:256]
        outs[j][2 * PIECE :, 256:] = keep_ref[tail:, 256:]


def four(terms):
    terms = [t.astype(F32) for t in terms]
    return (terms[0] + terms[1]) + (terms[2] + terms[3])


def chip_sum_kernel(*refs):
    refs[-1][...] = four([p[: 2 * PIECE, :] for p in refs[:CHIPS]]).astype(BF16)


def coupling_kernel(at_ref, *refs):
    parts, coup_ref = refs[:CHIPS], refs[-1]
    at = lax.broadcasted_iota(jnp.int32, (1, 128), 1)
    result = [jnp.zeros((1, 128), F32)] * 2
    for k in range(ROWS):
        half = slice(128 * (k % 2), 128 * (k % 2) + 128)
        packed = parts[k // 2][2 * PIECE :, half].astype(F32)
        for f in range(MINE):
            here = at == (at_ref[0] ^ k) * MINE + f
            for c in range(2):
                i = 2 * f + c
                value = packed[i : i + 1] + packed[4 + i : 5 + i] + packed[8 + i : 9 + i]
                result[c] = jnp.where(here, value, result[c])
    coup_ref[...] = jnp.concatenate(result, axis=0)[:, : ROWS * MINE]


def four_sum_kernel(*refs):
    refs[-1][...] = four([r[...] for r in refs[:4]]).astype(BF16)


def final_kernel(row_ref, *refs):
    over_ref, more_ref, *blocks, out_ref, mask_ref = refs
    over = over_ref[...].astype(F32) + more_ref[...].astype(F32)
    re, im = over[:PIECE], over[PIECE:]
    denom = jnp.maximum(jnp.sqrt(re * re + im * im), 1.0)
    re, im = re / denom, im / denom
    mask_ref[0] = re
    mask_ref[1] = im
    for k in range(ROWS):
        block = block_of(blocks, k)
        first = (row_ref[0] ^ k) * MINE
        for f in range(MINE):
            f_re = block[2 * f].astype(F32)
            f_im = block[2 * f + 1].astype(F32)
            out_ref[first + f, 0] = (f_re * re - f_im * im).astype(BF16)
            out_ref[first + f, 1] = (f_re * im + f_im * re).astype(BF16)


def cut_kernel(row_ref, fields_ref, keep_ref, give_ref):
    for k in range(ROWS):
        out = give_ref if k % 2 else keep_ref
        out[k // 2] = fields_ref[pl.ds((row_ref[0] ^ k) * 2 * MINE, 2 * MINE)]


def call(kernel, args, outs, scratch=(), flops=0, after=(), through=()):
    args, after = list(args), list(after) + list(through)
    first = len(args) + len(after) - len(through)
    alias = {first + i: len(outs) + i for i in range(len(through))}
    size = sum(a.size * a.dtype.itemsize for a in args) + sum(
        math.prod(s) * jnp.dtype(t).itemsize for s, t in outs
    )
    n, m = len(args), len(args) + len(after) + len(outs)

    def body(*refs):
        kernel(*refs[:n], *refs[n + len(after) : m], *refs[m + len(through) :])

    outputs = pl.pallas_call(
        body,
        name=kernel.__name__,
        out_shape=[jax.ShapeDtypeStruct(s, t) for s, t in outs]
        + [jax.ShapeDtypeStruct(t.shape, t.dtype) for t in through],
        in_specs=[SMEM if a.dtype == jnp.int32 else VMEM for a in args] + [ANY] * len(after),
        out_specs=[VMEM] * len(outs) + [ANY] * len(through),
        input_output_aliases=alias,
        scratch_shapes=[pltpu.VMEM(s, t) for s, t in scratch],
        compiler_params=pltpu.CompilerParams(vmem_limit_bytes=LIMIT),
        cost_estimate=pl.CostEstimate(flops=flops, bytes_accessed=size, transcendentals=0),
    )(*args, *after)
    return list(outputs)


def over_rows(block, k, name):
    with jax.named_scope(name):
        return lax.ppermute(block, "rows", [(s, s ^ k) for s in range(ROWS)])


def over_modes(block, k, name):
    with jax.named_scope(name):
        return lax.ppermute(block, "modes", [(s, s ^ k) for s in range(lax.axis_size("modes"))])


def both_cores(keep, give, name, more=()):
    got = over_rows(give, 1, name)
    pairs = [jnp.concatenate([keep[j], got[j], *more]) for j in range(1, CHIPS)]
    return keep, got, pairs


def shards(fwd_fields, bwd_fields, wavelength, kernel_phase, mask_phase):
    at = lax.axis_index("rows").astype(jnp.int32)[None]

    sent = ((CHIPS, 2 * MINE, PIECE, N), BF16)
    low_mask = mask_phase.astype(BF16)[None]
    keep, give = call(cut_kernel, [at, fwd_fields.reshape(-1, PIECE, N)], [sent] * 2)
    keep, got, pairs = both_cores(keep, give, "forward_entry_core", [low_mask])
    fwd_blocks = [keep, got] + [
        over_rows(p, 2 * j + 2, f"forward_entry_chip{j + 1}") for j, p in enumerate(pairs)
    ]
    masks = jnp.concatenate([low_mask] + [b[4 * MINE :] for b in fwd_blocks[2:]])
    (mask,) = call(
        mask_kernel, [at, masks, over_rows(masks, 1, "mask_core")], [((2, N, N), F32)]
    )

    wide = (2 * N, 2 * N)
    scratch = [(wide, BF16), (wide, BF16)]
    work = 2 * (2 * N) ** 3
    fore, back, keep, give = call(
        tables_kernel, [at, bwd_fields], [(wide, BF16), (wide, BF16), sent, sent], scratch, work
    )
    got = over_rows(give, 1, "backward_entry_core")
    trig, got = call(
        trig_kernel,
        [at, wavelength, kernel_phase],
        [((MINE, 2, N, N), F32)],
        after=fwd_blocks[2:3],
        through=[got],
    )
    (got,) = call(gate_kernel, [at], [], after=fwd_blocks[3:4], through=[got])
    pairs = [jnp.concatenate([keep[j], got[j]]) for j in range(1, CHIPS)]
    bwd_blocks = [keep, got] + [
        over_rows(p, 2 * j + 2, f"backward_entry_chip{j + 1}") for j, p in enumerate(pairs)
    ]

    space, keep, give = call(
        forward_kernel,
        [at, *fwd_blocks, fore, back, trig],
        [((MINE, N, 2 * N), F32), sent, sent],
        scratch,
        4 * work,
    )
    keep, got, pairs = both_cores(keep, give, "forward_exit_core")
    start1, pairs[1] = over_rows(keep[2], 4, "forward_exit_start2"), got[2]
    size = CHIPS * 2 * PIECE + 16
    over_keep, over_give = call(
        backward_kernel,
        [at, *bwd_blocks, fore, back, trig, space, mask],
        [((size, N), BF16), ((size, N), BF16)],
        scratch + [((2, N, N), BF16)],
        3 * work,
    )
    over_got = over_rows(over_give, 1, "over_core")
    sums = call(
        core_sum_kernel,
        [over_keep, over_got],
        [((2 * PIECE + 16, N), BF16)] * CHIPS,
        after=[got],
    )
    parts = [sums[0]] + [over_rows(sums[j], 2 * j, f"over_chip{j}") for j in range(1, CHIPS)]
    small = ((2 * PIECE, N), BF16)
    over, *pairs = call(chip_sum_kernel, parts, [small], after=[start1], through=pairs)
    (coupling,) = call(coupling_kernel, [at, *parts], [((2, ROWS * MINE), F32)])
    near, far, last = [
        over_rows(p, 2 * j + 2, f"forward_exit_chip{j + 1}") for j, p in enumerate(pairs)
    ]
    far = jnp.concatenate([start1, far])
    terms = [over] + [over_modes(over, k, f"over_x{k}") for k in X_STEPS]
    (over,) = call(four_sum_kernel, terms, [small])
    terms = [over] + [over_modes(over, k, f"over_y{k // 8}") for k in Y_STEPS]
    (over,) = call(four_sum_kernel, terms, [small], after=[far, coupling])
    fwd_out, new_mask = call(
        final_kernel,
        [at, over, over_modes(over, Z_STEP, "over_z"), keep, got, near, far, last],
        [((ROWS * MINE, 2, PIECE, N), BF16), ((2, PIECE, N), F32)],
    )
    return fwd_out, new_mask, coupling


def solution(mesh):
    in_specs = (
        P("modes", None, "rows", None),
        P("modes", None, "rows", None),
        P("modes"),
        P(),
        P("rows", None),
    )
    out_specs = (P("modes", None, "rows", None), P(None, "rows", None), P(None, "modes"))
    return jax.shard_map(shards, mesh=mesh, in_specs=in_specs, out_specs=out_specs, check_vma=False)
```

```python
import math

import jax
import jax.numpy as jnp
from jax import lax
from jax.experimental import pallas as pl
from jax.experimental.pallas import tpu as pltpu
from jax.sharding import PartitionSpec as P

N = 384
ROWS = 8
CHIPS = 4
PIECE = N // ROWS
MINE = 2
FIELDS = 512
X_STEPS = (1, 2, 3)
Y_STEPS = (8, 16, 24)
Z_STEP = 4
SMEM = pl.BlockSpec(memory_space=pltpu.SMEM)
VMEM = pl.BlockSpec(memory_space=pltpu.VMEM)
ANY = pl.BlockSpec(memory_space=pl.ANY)
LIMIT = 16 * 1024 * 1024
BF16, F32 = jnp.bfloat16, jnp.float32


def sincos(angle):
    y = angle * 0.5
    z = y * y
    s = -1.0 / 39916800.0
    for c in (1.0 / 362880.0, -1.0 / 5040.0, 1.0 / 120.0, -1.0 / 6.0, 1.0):
        s = s * z + c
    s = s * y
    c = 1.0 / 479001600.0
    for d in (-1.0 / 3628800.0, 1.0 / 40320.0, -1.0 / 720.0, 1.0 / 24.0, -0.5, 1.0):
        c = c * z + d
    return 1.0 - 2.0 * s * s, 2.0 * s * c


def dot(a, b):
    return jnp.dot(a, b, preferred_element_type=F32)


def lanes(i):
    return slice(i * N, (i + 1) * N)


def tables_kernel(row_ref, fields_ref, fore_ref, back_ref, keep_ref, give_ref, one, two):
    for r in range(0, N, 128):
        j = lax.broadcasted_iota(jnp.int32, (128, N), 0) + r
        k = lax.broadcasted_iota(jnp.int32, (128, N), 1)
        jk = (j * k).astype(F32)
        turn = jnp.floor(jk * (1.0 / N) + 0.5)
        cosine, sine = sincos((jk - turn * N) * (2.0 * math.pi / N))
        scale = 1.0 / math.sqrt(N)
        cosine = (cosine * scale).astype(BF16)
        sine = (sine * scale).astype(BF16)
        a, b = pl.ds(r, 128), pl.ds(N + r, 128)
        fore_ref[a, :N] = cosine
        fore_ref[a, N:] = -sine
        fore_ref[b, :N] = sine
        fore_ref[b, N:] = cosine
        back_ref[a, :N] = cosine
        back_ref[a, N:] = sine
        back_ref[b, :N] = -sine
        back_ref[b, N:] = cosine
    for f in range(ROWS * MINE):
        for c in range(2):
            one[f * PIECE : (f + 1) * PIECE, lanes(c)] = fields_ref[f, c]
    for h in range(2):
        two[lanes(h), :] = dot(one[lanes(h), :], fore_ref[...]).astype(BF16)
    for k in range(ROWS):
        out = give_ref if k % 2 else keep_ref
        for f in range(MINE):
            top = pl.multiple_of(((row_ref[0] ^ k) * MINE + f) * PIECE, 16)
            for c in range(2):
                out[k // 2, 2 * f + c] = two[pl.ds(top, PIECE), lanes(c)]


def gate_kernel(row_ref):
    del row_ref


def trig_kernel(row_ref, wave_ref, phase_ref, trig_ref):
    for f in range(MINE):
        wave = wave_ref[row_ref[0] * MINE + f]
        for r in range(0, N, 128):
            cosine, sine = sincos(phase_ref[wave, pl.ds(r, 128), :])
            trig_ref[f, 0, pl.ds(r, 128), :] = cosine
            trig_ref[f, 1, pl.ds(r, 128), :] = sine


def mask_kernel(row_ref, mine_ref, got_ref, mask_ref):
    for k in range(ROWS):
        piece = (got_ref if k % 2 else mine_ref)[k // 2]
        top = pl.multiple_of((row_ref[0] ^ k) * PIECE, 16)
        cosine, sine = sincos(piece.astype(F32))
        mask_ref[0, pl.ds(top, PIECE), :] = cosine
        mask_ref[1, pl.ds(top, PIECE), :] = sine


def spectral(sign, fore_ref, back_ref, trig_ref, one, two):
    for c in range(2):
        one[lanes(c), :] = dot(back_ref[lanes(c), :], two[...]).astype(BF16)
    for f in range(MINE):
        re = one[:N, lanes(f)].astype(F32)
        im = one[N:, lanes(f)].astype(F32)
        cosine, sine = trig_ref[f, 0], sign * trig_ref[f, 1]
        two[:N, lanes(f)] = (cosine * re - sine * im).astype(BF16)
        two[N:, lanes(f)] = (sine * re + cosine * im).astype(BF16)
    for c in range(2):
        d = dot(fore_ref[lanes(c), :], two[...]).astype(BF16)
        for f in range(MINE):
            one[lanes(f), lanes(c)] = d[:, lanes(f)]
    return [dot(one[lanes(f), :], back_ref[...]) for f in range(MINE)]


def block_of(blocks, k):
    if k < 2:
        return blocks[k].at[0]
    return blocks[1 + k // 2].at[pl.ds(k % 2 * 2 * MINE, 2 * MINE)]


def forward_kernel(*refs):
    row_ref, blocks = refs[0], refs[1 : 2 + CHIPS]
    fore_ref, back_ref, trig_ref, space_ref, keep_ref, give_ref, one, two = refs[2 + CHIPS :]
    for k in range(ROWS):
        block = block_of(blocks, k)
        top = pl.multiple_of((row_ref[0] ^ k) * PIECE, 16)
        for f in range(MINE):
            for c in range(2):
                one[pl.ds(f * N + top, PIECE), lanes(c)] = block[2 * f + c]
    for f in range(MINE):
        a = dot(one[lanes(f), :], fore_ref[...]).astype(BF16)
        two[:N, lanes(f)] = a[:, :N]
        two[N:, lanes(f)] = a[:, N:]
    space = spectral(1.0, fore_ref, back_ref, trig_ref, one, two)
    for f in range(MINE):
        space_ref[f] = space[f]
        two[lanes(f), :] = space[f].astype(BF16)
    for k in range(ROWS):
        out = give_ref if k % 2 else keep_ref
        top = pl.multiple_of((row_ref[0] ^ k) * PIECE, 16)
        for f in range(MINE):
            for c in range(2):
                out[k // 2, 2 * f + c] = two[pl.ds(f * N + top, PIECE), lanes(c)]


def total(x):
    return jnp.sum(jnp.sum(x, axis=0, keepdims=True), axis=1, keepdims=True)


def backward_kernel(*refs):
    row_ref, blocks = refs[0], refs[1 : 2 + CHIPS]
    fore_ref, back_ref, trig_ref, space_ref, mask_ref = refs[2 + CHIPS : 7 + CHIPS]
    keep_ref, give_ref, one, two, over = refs[7 + CHIPS :]
    for k in range(ROWS):
        block = block_of(blocks, k)
        top = pl.multiple_of((row_ref[0] ^ k) * PIECE, 16)
        for f in range(MINE):
            for c in range(2):
                two[pl.ds(c * N + top, PIECE), lanes(f)] = block[2 * f + c]
    space = spectral(-1.0, fore_ref, back_ref, trig_ref, one, two)
    cosine, sine = mask_ref[0], mask_ref[1]
    over_re, over_im = 0.0, 0.0
    rows = []
    for f in range(MINE):
        b_re, b_im = space[f][:, :N], space[f][:, N:]
        f_re, f_im = space_ref[f, :, :N], space_ref[f, :, N:]
        g_re = f_re * b_re + f_im * b_im
        g_im = f_im * b_re - f_re * b_im
        c_re = total(g_re * cosine - g_im * sine) * (1.0 / N)
        c_im = total(g_re * sine + g_im * cosine) * (1.0 / N)
        over_re = over_re + (g_re * c_re + g_im * c_im)
        over_im = over_im + (g_im * c_re - g_re * c_im)
        rows += [c_re, c_im]
    scale = 1.0 / math.sqrt(FIELDS)
    over[0] = (over_re * scale).astype(BF16)
    over[1] = (over_im * scale).astype(BF16)
    for k in range(ROWS):
        out = give_ref if k % 2 else keep_ref
        top = pl.multiple_of((row_ref[0] ^ k) * PIECE, 16)
        for c in range(2):
            start = ((k // 2) * 2 + c) * PIECE
            out[start : start + PIECE, :] = over[c, pl.ds(top, PIECE), :]
    high = [r.astype(BF16) for r in rows]
    rest = [r - h.astype(F32) for r, h in zip(rows, high)]
    mid = [r.astype(BF16) for r in rest]
    low = [(r - m.astype(F32)).astype(BF16) for r, m in zip(rest, mid)]
    at = lax.broadcasted_iota(jnp.int32, (16, N), 0)
    packed = jnp.zeros((16, N), F32)
    for t, terms in enumerate((high, mid, low)):
        for i, value in enumerate(terms):
            packed = jnp.where(at == 4 * t + i, value.astype(F32), packed)
    for out in (keep_ref, give_ref):
        out[CHIPS * 2 * PIECE :, :] = packed.astype(BF16)


def core_sum_kernel(keep_ref, got_ref, *outs):
    tail = CHIPS * 2 * PIECE
    for j in range(CHIPS):
        at = slice(j * 2 * PIECE, (j + 1) * 2 * PIECE)
        both = keep_ref[at, :].astype(F32) + got_ref[at, :].astype(F32)
        outs[j][: 2 * PIECE, :] = both.astype(BF16)
        outs[j][2 * PIECE :, :128] = keep_ref[tail:, :128]
        outs[j][2 * PIECE :, 128:256] = got_ref[tail:, 128:256]
        outs[j][2 * PIECE :, 256:] = keep_ref[tail:, 256:]


def four(terms):
    terms = [t.astype(F32) for t in terms]
    return (terms[0] + terms[1]) + (terms[2] + terms[3])


def chip_sum_kernel(at_ref, *refs):
    parts, (over_ref, coup_ref) = refs[:CHIPS], refs[-2:]
    over_ref[...] = four([p[: 2 * PIECE, :] for p in parts]).astype(BF16)
    at = lax.broadcasted_iota(jnp.int32, (1, 128), 1)
    result = [jnp.zeros((1, 128), F32)] * 2
    for k in range(ROWS):
        half = slice(128 * (k % 2), 128 * (k % 2) + 128)
        packed = parts[k // 2][2 * PIECE :, half].astype(F32)
        for f in range(MINE):
            here = at == (at_ref[0] ^ k) * MINE + f
            for c in range(2):
                i = 2 * f + c
                value = packed[i : i + 1] + packed[4 + i : 5 + i] + packed[8 + i : 9 + i]
                result[c] = jnp.where(here, value, result[c])
    coup_ref[...] = jnp.concatenate(result, axis=0)[:, : ROWS * MINE]


def four_sum_kernel(*refs):
    refs[-1][...] = four([r[...] for r in refs[:4]]).astype(BF16)


def final_kernel(row_ref, *refs):
    over_ref, more_ref, *blocks, out_ref, mask_ref = refs
    over = over_ref[...].astype(F32) + more_ref[...].astype(F32)
    re, im = over[:PIECE], over[PIECE:]
    denom = jnp.maximum(jnp.sqrt(re * re + im * im), 1.0)
    re, im = re / denom, im / denom
    mask_ref[0] = re
    mask_ref[1] = im
    for k in range(ROWS):
        block = block_of(blocks, k)
        first = (row_ref[0] ^ k) * MINE
        for f in range(MINE):
            f_re = block[2 * f].astype(F32)
            f_im = block[2 * f + 1].astype(F32)
            out_ref[first + f, 0] = (f_re * re - f_im * im).astype(BF16)
            out_ref[first + f, 1] = (f_re * im + f_im * re).astype(BF16)


def cut_kernel(row_ref, fields_ref, keep_ref, give_ref):
    for k in range(ROWS):
        out = give_ref if k % 2 else keep_ref
        out[k // 2] = fields_ref[pl.ds((row_ref[0] ^ k) * 2 * MINE, 2 * MINE)]


def call(kernel, args, outs, scratch=(), flops=0, after=(), through=()):
    args, after = list(args), list(after) + list(through)
    first = len(args) + len(after) - len(through)
    alias = {first + i: len(outs) + i for i in range(len(through))}
    size = sum(a.size * a.dtype.itemsize for a in args) + sum(
        math.prod(s) * jnp.dtype(t).itemsize for s, t in outs
    )
    n, m = len(args), len(args) + len(after) + len(outs)

    def body(*refs):
        kernel(*refs[:n], *refs[n + len(after) : m], *refs[m + len(through) :])

    outputs = pl.pallas_call(
        body,
        name=kernel.__name__,
        out_shape=[jax.ShapeDtypeStruct(s, t) for s, t in outs]
        + [jax.ShapeDtypeStruct(t.shape, t.dtype) for t in through],
        in_specs=[SMEM if a.dtype == jnp.int32 else VMEM for a in args] + [ANY] * len(after),
        out_specs=[VMEM] * len(outs) + [ANY] * len(through),
        input_output_aliases=alias,
        scratch_shapes=[pltpu.VMEM(s, t) for s, t in scratch],
        compiler_params=pltpu.CompilerParams(vmem_limit_bytes=LIMIT),
        cost_estimate=pl.CostEstimate(flops=flops, bytes_accessed=size, transcendentals=0),
    )(*args, *after)
    return list(outputs)


def over_rows(block, k, name):
    with jax.named_scope(name):
        return lax.ppermute(block, "rows", [(s, s ^ k) for s in range(ROWS)])


def over_modes(block, k, name):
    with jax.named_scope(name):
        return lax.ppermute(block, "modes", [(s, s ^ k) for s in range(lax.axis_size("modes"))])


def both_cores(keep, give, name, more=()):
    got = over_rows(give, 1, name)
    pairs = [jnp.concatenate([keep[j], got[j], *more]) for j in range(1, CHIPS)]
    return keep, got, pairs


def shards(fwd_fields, bwd_fields, wavelength, kernel_phase, mask_phase):
    at = lax.axis_index("rows").astype(jnp.int32)[None]

    sent = ((CHIPS, 2 * MINE, PIECE, N), BF16)
    low_mask = mask_phase.astype(BF16)[None]
    keep, give = call(cut_kernel, [at, fwd_fields.reshape(-1, PIECE, N)], [sent] * 2)
    keep, got, pairs = both_cores(keep, give, "forward_entry_core", [low_mask])
    fwd_blocks = [keep, got] + [
        over_rows(p, 2 * j + 2, f"forward_entry_chip{j + 1}") for j, p in enumerate(pairs)
    ]
    masks = jnp.concatenate([low_mask] + [b[4 * MINE :] for b in fwd_blocks[2:]])
    (mask,) = call(
        mask_kernel, [at, masks, over_rows(masks, 1, "mask_core")], [((2, N, N), F32)]
    )

    wide = (2 * N, 2 * N)
    scratch = [(wide, BF16), (wide, BF16)]
    work = 2 * (2 * N) ** 3
    fore, back, keep, give = call(
        tables_kernel, [at, bwd_fields], [(wide, BF16), (wide, BF16), sent, sent], scratch, work
    )
    got = over_rows(give, 1, "backward_entry_core")
    trig, got = call(
        trig_kernel,
        [at, wavelength, kernel_phase],
        [((MINE, 2, N, N), F32)],
        after=fwd_blocks[2:3],
        through=[got],
    )
    (got,) = call(gate_kernel, [at], [], after=fwd_blocks[3:4], through=[got])
    pairs = [jnp.concatenate([keep[j], got[j]]) for j in range(1, CHIPS)]
    bwd_blocks = [keep, got] + [
        over_rows(p, 2 * j + 2, f"backward_entry_chip{j + 1}") for j, p in enumerate(pairs)
    ]

    space, keep, give = call(
        forward_kernel,
        [at, *fwd_blocks, fore, back, trig],
        [((MINE, N, 2 * N), F32), sent, sent],
        scratch,
        4 * work,
    )
    keep, got, pairs = both_cores(keep, give, "forward_exit_core")
    start1, pairs[1] = over_rows(keep[2], 4, "forward_exit_start2"), got[2]
    size = CHIPS * 2 * PIECE + 16
    over_keep, over_give = call(
        backward_kernel,
        [at, *bwd_blocks, fore, back, trig, space, mask],
        [((size, N), BF16), ((size, N), BF16)],
        scratch + [((2, N, N), BF16)],
        3 * work,
    )
    over_got = over_rows(over_give, 1, "over_core")
    sums = call(
        core_sum_kernel,
        [over_keep, over_got],
        [((2 * PIECE + 16, N), BF16)] * CHIPS,
        after=[got],
    )
    parts = [sums[0]] + [over_rows(sums[j], 2 * j, f"over_chip{j}") for j in range(1, CHIPS)]
    small = ((2 * PIECE, N), BF16)
    over, coupling, *pairs = call(
        chip_sum_kernel,
        [at, *parts],
        [small, ((2, ROWS * MINE), F32)],
        after=[start1],
        through=pairs,

    )
    near, far, last = [
        over_rows(p, 2 * j + 2, f"forward_exit_chip{j + 1}") for j, p in enumerate(pairs)
    ]
    far = jnp.concatenate([start1, far])
    terms = [over] + [over_modes(over, k, f"over_x{k}") for k in X_STEPS]
    (over,) = call(four_sum_kernel, terms, [small])
    terms = [over] + [over_modes(over, k, f"over_y{k // 8}") for k in Y_STEPS]
    (over,) = call(four_sum_kernel, terms, [small], after=[far])
    fwd_out, new_mask = call(
        final_kernel,
        [at, over, over_modes(over, Z_STEP, "over_z"), keep, got, near, far, last],
        [((ROWS * MINE, 2, PIECE, N), BF16), ((2, PIECE, N), F32)],
    )
    return fwd_out, new_mask, coupling


def solution(mesh):
    in_specs = (
        P("modes", None, "rows", None),
        P("modes", None, "rows", None),
        P("modes"),
        P(),
        P("rows", None),
    )
    out_specs = (P("modes", None, "rows", None), P(None, "rows", None), P(None, "modes"))
    return jax.shard_map(shards, mesh=mesh, in_specs=in_specs, out_specs=out_specs, check_vma=False)
```
